32 devices in a mesh: groups: 2 (over x), expert: 16 (over z, y, core).
Axes of the slice: x: 2, y: 2, z: 4, core: 2. Of those that a mesh axis runs over, the one named last changes fastest.
Arguments:
- tokens: bfloat16 [4096, 7168], P(('groups', 'expert')), parts along dimension 0, may hold values from -6 to 6
- out_grad: bfloat16 [4096, 7168], P(('groups', 'expert')), parts along dimension 0, may hold values from -6 to 6
- routes: int32 [4096, 8], P(('groups', 'expert')), parts along dimension 0, may hold values from 0 to 255, as said below
- gate_probs: float32 [4096, 8], P(('groups', 'expert')), parts along dimension 0, may hold values from 0.1 to 1
- w_gate: bfloat16 [7168, 2048], P(None, 'expert'), may hold values from -0.0625 to 0.0625
- w_up: bfloat16 [7168, 2048], P(None, 'expert'), may hold values from -0.0625 to 0.0625
- w_down: bfloat16 [2048, 7168], P('expert'), may hold values from -0.125 to 0.125
Outputs:
- layer_out: bfloat16 [4096, 7168], P(('groups', 'expert')), parts along dimension 0
- input_grad: bfloat16 [4096, 7168], P(('groups', 'expert')), parts along dimension 0
- prob_grad: float32 [4096, 8], P(('groups', 'expert')), parts along dimension 0
The draws below stay inside these ranges and needn't reach their ends.
There are 2 independent parts, one for each index of `groups`. The reference program is written for one: setup_inputs(seed, part) draws one part's arguments, and reference() takes and returns one part's arrays. A program takes and returns all parts, laid end to end along the dimension named above; an argument that names none is the same for every part. Nothing has to cross between parts.
Inputs may be any that keep to these rules, and one draw needn't show every extreme that they name: `routes`: each row names 8 different experts. Among the 128 rows of one device, each expert id below 1 is named by 1 to 4 rows. In every draw each id below 1 is named by exactly 4 rows on some device, and some id below 1 is named by exactly 4 rows on every device.
All inputs are finite; a program needn't handle non-finite values.
Results may differ from the reference program's by a relative error of at most 0.0057.
Values may be sent and summed in bfloat16 or wider, within the bound.
No kernel may reach another device: no remote copies, remote signals or barrier semaphores. Data moves between devices by JAX's collectives and lax.ppermute only.
A program may use at most 64 MiB of HBM per device.

```python
import jax
import jax.numpy as jnp
from jax import lax

D = 7168
HID = 2048
N_ROUTED = 256
TOPK = 8
PANEL = 128
CAP = 4
TOK_DEV = 128
EXPERTS = 1
TOKENS = 2048
N_EXPERT = 16


def draw_routes(key, part):
    key = jax.random.fold_in(key, 11)
    panels = HID // PANEL
    experts = N_EXPERT // panels
    hot_key, raise_key, level_key, shift_key, pick_key, other_key = jax.random.split(key, 6)
    expert_ids = jnp.arange(experts, dtype=jnp.int32)
    device_ids = jnp.arange(N_EXPERT, dtype=jnp.int32)
    hottest = jax.random.randint(hot_key, (), 0, experts)
    raised = jax.random.randint(raise_key, (N_EXPERT, experts), 0, 8) == 0
    levels = jax.random.randint(level_key, (N_EXPERT, experts), 2, CAP + 1)
    counts = jnp.where(raised, levels, 1)
    offset = jax.random.randint(shift_key, (), 0, N_EXPERT)
    forced = (device_ids + offset) % N_EXPERT
    counts = jnp.where(forced[:, None] == expert_ids[None, :], CAP, counts)
    counts = jnp.where(expert_ids[None, :] == hottest, CAP, counts)
    picks = jax.random.randint(pick_key, (N_EXPERT, experts, TOK_DEV), 0, 1 << 20)
    distinct = picks * TOK_DEV + jnp.arange(TOK_DEV, dtype=jnp.int32)[None, None, :]
    ranking = jnp.argsort(jnp.argsort(distinct, axis=2), axis=2)
    chosen = ranking < counts[:, :, None]
    chosen = jnp.transpose(chosen, (0, 2, 1)).reshape(TOKENS, experts)
    chosen_full = jnp.pad(chosen, ((0, 0), (0, N_ROUTED - experts)))
    others = jax.random.randint(other_key, (TOKENS, N_ROUTED), 0, 1 << 20)
    scores = others * N_ROUTED + jnp.arange(N_ROUTED, dtype=jnp.int32)[None, :]
    inside = jnp.arange(N_ROUTED)[None, :] < experts
    scores = jnp.where(inside, jnp.where(chosen_full, 1 << 30, -1), scores)
    picked = lax.top_k(scores, TOPK)[1]
    return picked.astype(jnp.int32)


def shard_levels(rng, shape, pieces, least, high):
    loudness, own = 1.0, jax.random.fold_in(rng, 6)
    for dim, shards_of in pieces:
        steps = jnp.exp(jax.random.uniform(jax.random.fold_in(own, dim), (shards_of,), jnp.float32, least / len(pieces), high / len(pieces)))
        loudness = loudness * jnp.repeat(steps, shape[dim] // shards_of).reshape([-1 if axis == dim else 1 for axis in range(len(shape))])
    return loudness


def normal_values(rng, dims, width, bound, cuts=(), held_as=jnp.bfloat16):
    factor_of = shard_levels(rng, dims, cuts, -0.22, 0.18) if cuts else 1.0
    values = jax.random.normal(rng, dims, jnp.float32) * width * factor_of
    return jnp.minimum(jnp.maximum(values, -bound), bound).astype(held_as)


def setup_inputs(seed: int = 0, part: int = 0) -> dict:
    key_list = jax.random.split(jax.random.key(seed), 8)
    part_keys = jax.random.split(jax.random.fold_in(key_list[7], part), 8)
    return {
        "tokens": normal_values(part_keys[0], (TOKENS, D), 1.0, 6.0, ((0, 16),)),
        "out_grad": normal_values(part_keys[1], (TOKENS, D), 1.0, 6.0, ((0, 16),)),
        "routes": draw_routes(jax.random.fold_in(jax.random.fold_in(key_list[7], part), 71), part),
        "gate_probs": jnp.clip(0.1 + 0.9 * jax.random.uniform(part_keys[3], (TOKENS, TOPK), jnp.float32) ** shard_levels(part_keys[3], (TOKENS, TOPK), ((0, 16),), -0.2, 0.2), 0.1, 1.0),
        "w_gate": normal_values(key_list[4], (D, EXPERTS * HID), D ** -0.5, 0.0625, ((1, 16),)),
        "w_up": normal_values(key_list[5], (D, EXPERTS * HID), D ** -0.5, 0.0625, ((1, 16),)),
        "w_down": normal_values(key_list[6], (EXPERTS * HID, D), HID ** -0.5, 0.125, ((0, 16),)),
    }


def reference(tokens, out_grad, routes, gate_probs, w_gate, w_up, w_down):
    panels = HID // PANEL
    experts = N_EXPERT // panels
    slot_total = N_EXPERT * CAP
    layer_acc = tokens.astype(jnp.float32)
    grad_acc = out_grad.astype(jnp.float32)
    prob_grad = jnp.zeros((TOKENS, TOPK), jnp.float32)
    zero_row = jnp.zeros((1, D), jnp.bfloat16)
    padded_tokens = jnp.concatenate([tokens, zero_row], axis=0)
    padded_grads = jnp.concatenate([out_grad, zero_row], axis=0)
    for expert in range(experts):
        matches = routes == expert
        is_hit = jnp.any(matches, axis=1)
        prob_each = jnp.sum(jnp.where(matches, gate_probs, 0.0), axis=1)
        prob_padded = jnp.concatenate([prob_each, jnp.zeros((1,), jnp.float32)])
        row_index = jnp.nonzero(is_hit, size=slot_total, fill_value=TOKENS)[0].astype(jnp.int32)
        token_rows = padded_tokens[row_index]
        grad_rows = padded_grads[row_index]
        row_prob = prob_padded[row_index]
        weighted = (row_prob[:, None] * grad_rows.astype(jnp.float32)).astype(jnp.bfloat16)
        gate_cols = w_gate[:, expert * HID:(expert + 1) * HID]
        up_cols = w_up[:, expert * HID:(expert + 1) * HID]
        down_rows = w_down[expert * HID:(expert + 1) * HID, :]
        gate_pre = jnp.dot(token_rows, gate_cols, preferred_element_type=jnp.float32)
        up_pre = jnp.dot(token_rows, up_cols, preferred_element_type=jnp.float32)
        sigmoid_gate = jax.nn.sigmoid(gate_pre)
        silu_gate = gate_pre * sigmoid_gate
        hidden = (silu_gate * up_pre).astype(jnp.bfloat16)
        hidden_panels = hidden.reshape(slot_total, panels, PANEL).astype(jnp.float32)
        down_panels = down_rows.reshape(panels, PANEL, D).astype(jnp.float32)
        out_parts = jnp.einsum("rpk,pkd->prd", hidden_panels, down_panels).astype(jnp.bfloat16)
        out_parts = lax.optimization_barrier(out_parts)
        expert_out = jnp.sum(out_parts.astype(jnp.float32), axis=0)
        contract = (((1,), (1,)), ((), ()))
        hidden_grad = lax.dot_general(weighted, down_rows, contract, preferred_element_type=jnp.float32)
        silu_slope = sigmoid_gate * (1.0 + gate_pre * (1.0 - sigmoid_gate))
        gate_grad = (hidden_grad * up_pre * silu_slope).astype(jnp.bfloat16)
        up_grad = (hidden_grad * silu_gate).astype(jnp.bfloat16)
        gate_grad3 = gate_grad.reshape(slot_total, panels, PANEL).astype(jnp.float32)
        up_grad3 = up_grad.reshape(slot_total, panels, PANEL).astype(jnp.float32)
        gate_cols3 = gate_cols.reshape(D, panels, PANEL).astype(jnp.float32)
        up_cols3 = up_cols.reshape(D, panels, PANEL).astype(jnp.float32)
        input_parts = jnp.einsum("rpk,dpk->prd", gate_grad3, gate_cols3) + jnp.einsum("rpk,dpk->prd", up_grad3, up_cols3)
        input_parts = lax.optimization_barrier(input_parts.astype(jnp.bfloat16))
        input_sum = jnp.sum(input_parts.astype(jnp.float32), axis=0)
        layer_acc = layer_acc.at[row_index].add(row_prob[:, None] * expert_out, mode="drop")
        grad_acc = grad_acc.at[row_index].add(input_sum, mode="drop")
        slot_dot = jnp.sum(grad_rows.astype(jnp.float32) * expert_out, axis=1)
        token_dot = jnp.zeros((TOKENS,), jnp.float32).at[row_index].add(slot_dot, mode="drop")
        prob_grad = prob_grad + jnp.where(matches, token_dot[:, None], 0.0)
    return layer_acc.astype(jnp.bfloat16), grad_acc.astype(jnp.bfloat16), prob_grad
```

```python
import jax
import jax.numpy as jnp
from jax import lax
from jax.sharding import PartitionSpec as P

HID = 2048
PANEL = 128
CAP = 4
PANELS = HID // PANEL
AXIS = "expert"

f32 = jnp.float32
bf16 = jnp.bfloat16


def slot_tables(routes, gate_probs, experts):
    expert_ids = jnp.arange(experts, dtype=jnp.int32)
    matches = routes[:, :, None] == expert_ids[None, None, :]
    per_token = jnp.sum(matches.astype(jnp.int32), axis=1)
    slot_order = jnp.cumsum(per_token, axis=0) - per_token
    slot_ids = jnp.arange(CAP, dtype=jnp.int32)
    placement = (per_token[:, :, None] == 1) & (slot_order[:, :, None] == slot_ids[None, None, :])
    placement = placement.astype(f32)
    route_prob = jnp.sum(jnp.where(matches, gate_probs[:, :, None], 0.0), axis=1)
    slot_prob = jnp.sum(placement * route_prob[:, :, None], axis=0).reshape(-1)
    return (matches, placement, slot_prob)


def swap(x, offset):
    devices = lax.axis_size(AXIS)
    return lax.ppermute(x, AXIS, [(i, i ^ offset) for i in range(devices)])


def gather_rows(x):
    blocks = {0: x}
    for far in range(PANELS // 4 - 1, 0, -1):
        blocks[4 * far] = swap(x, 4 * far)
    for far in range(PANELS // 4):
        blocks[4 * far + 2] = swap(blocks[4 * far], 2)
    even = jnp.stack([blocks[k] for k in range(0, PANELS, 2)])
    return even, swap(even, 1)


def scatter_sum(even, odd):
    part = even.astype(f32) + swap(odd, 1).astype(f32)
    own = {}
    for far in range(PANELS // 4 - 1, -1, -1):
        own[far] = part[2 * far] + swap(part[2 * far + 1].astype(bf16), 2).astype(f32)
    total = own[0]
    for far in range(PANELS // 4 - 1, 0, -1):
        total = total + swap(own[far].astype(bf16), 4 * far).astype(f32)
    return total


def expert_compute(token_rows, grad_rows, w_gate, w_up, w_down):
    gate_pre = jnp.dot(token_rows, w_gate, preferred_element_type=f32)
    up_pre = jnp.dot(token_rows, w_up, preferred_element_type=f32)
    sigmoid_gate = jax.nn.sigmoid(gate_pre)
    silu_gate = gate_pre * sigmoid_gate
    hidden = (silu_gate * up_pre).astype(bf16)
    expert_out = jnp.dot(hidden, w_down, preferred_element_type=f32).astype(bf16)
    contract = (((1,), (1,)), ((), ()))
    hidden_grad = lax.dot_general(grad_rows, w_down, contract, preferred_element_type=f32)
    silu_slope = sigmoid_gate * (1.0 + gate_pre * (1.0 - sigmoid_gate))
    gate_grad = (hidden_grad * up_pre * silu_slope).astype(bf16)
    up_grad = (hidden_grad * silu_gate).astype(bf16)
    input_part = lax.dot_general(gate_grad, w_gate, contract, preferred_element_type=f32)
    input_part = input_part + lax.dot_general(up_grad, w_up, contract, preferred_element_type=f32)
    return (expert_out, input_part.astype(bf16))


def local(tokens, out_grad, routes, gate_probs, w_gate, w_up, w_down):
    devices = lax.axis_size(AXIS)
    experts = devices // PANELS
    tok_count, width = tokens.shape
    slot_total = experts * CAP
    matches, placement, slot_prob = slot_tables(routes, gate_probs, experts)
    placement_flat = placement.reshape(tok_count, slot_total)
    picker = placement_flat.T.astype(bf16)
    token_slots = jnp.dot(picker, tokens, preferred_element_type=f32).astype(bf16)
    grad_slots = jnp.dot(picker, out_grad, preferred_element_type=f32).astype(bf16)
    weighted_slots = (slot_prob[:, None] * grad_slots.astype(f32)).astype(bf16)

    send = jnp.concatenate(
        [token_slots.reshape(experts, CAP, width), weighted_slots.reshape(experts, CAP, width)], axis=1
    )
    rows = 2 * CAP * experts
    peers = [[e * PANELS + r for e in range(experts)] for r in range(PANELS)]
    if experts > 1:
        send = lax.all_to_all(send, AXIS, 0, 0, axis_index_groups=peers, tiled=True)
    even, odd = gather_rows(send.reshape(rows, width))
    everyone = jnp.stack([even, odd]).reshape(-1, 2, CAP, width)
    out_rows, input_rows = expert_compute(
        everyone[:, 0].reshape(-1, width), everyone[:, 1].reshape(-1, width), w_gate, w_up, w_down
    )
    back = jnp.stack([out_rows.reshape(-1, CAP, width), input_rows.reshape(-1, CAP, width)], axis=1)
    back = back.reshape(2, PANELS // 2, rows, width)
    total = scatter_sum(back[0], back[1]).reshape(experts, 2 * CAP, width)
    if experts > 1:
        total = lax.all_to_all(total, AXIS, 0, 0, axis_index_groups=peers, tiled=True)
    out_sum = total[:, :CAP].reshape(slot_total, width)
    input_sum = total[:, CAP:].reshape(slot_total, width)

    highest = lax.Precision.HIGHEST
    mixing = placement_flat * slot_prob[None, :]
    layer_moe = jnp.dot(mixing, out_sum, precision=highest, preferred_element_type=f32)
    layer_out = (tokens.astype(f32) + layer_moe).astype(bf16)
    input_moe = jnp.dot(placement_flat, input_sum, precision=highest, preferred_element_type=f32)
    input_grad = (out_grad.astype(f32) + input_moe).astype(bf16)
    slot_dot = jnp.sum(grad_slots.astype(f32) * out_sum, axis=1)
    token_dot = jnp.sum(placement * slot_dot.reshape(experts, CAP)[None, :, :], axis=2)
    prob_grad = jnp.sum(jnp.where(matches, token_dot[:, None, :], 0.0), axis=2)
    return (layer_out, input_grad, prob_grad)


def solution(mesh):
    rows = P(("groups", AXIS), None)
    return jax.shard_map(
        local,
        mesh=mesh,
        in_specs=(rows, rows, rows, rows, P(None, AXIS), P(None, AXIS), P(AXIS, None)),
        out_specs=(rows, rows, rows),
        check_vma=False,
    )
```

```python
import functools

import jax
import jax.numpy as jnp
from jax import lax
from jax.experimental import pallas as pl
from jax.experimental.pallas import tpu as pltpu
from jax.sharding import PartitionSpec as P

HID = 2048
PANEL = 128
CAP = 4
PANELS = HID // PANEL
PAIR = 2 * CAP
AXIS = "expert"
MIB = 1 << 20

f32 = jnp.float32
bf16 = jnp.bfloat16
NT = (((1,), (1,)), ((), ()))
TN = (((0,), (0,)), ((), ()))


def chunk_of(width, most):
    return max(c for c in range(128, most + 1, 128) if width % c == 0)


def swap(x, offset):
    devices = lax.axis_size(AXIS)
    return lax.ppermute(x, AXIS, [(i, i ^ offset) for i in range(devices)])


def gather_rows(x):
    blocks = {0: x}
    for far in range(PANELS // 4 - 1, 0, -1):
        blocks[4 * far] = swap(x, 4 * far)
    for far in range(PANELS // 4):
        blocks[4 * far + 2] = swap(blocks[4 * far], 2)
    even = jnp.concatenate([blocks[k] for k in range(0, PANELS, 2)], axis=0)
    return even, swap(even, 1)


def scatter_sum(even, odd):
    rows = even.shape[0] // (PANELS // 2)
    part = (even.astype(f32) + swap(odd, 1).astype(f32)).reshape(PANELS // 2, rows, -1)
    own = {}
    for far in range(PANELS // 4 - 1, -1, -1):
        own[far] = part[2 * far] + swap(part[2 * far + 1].astype(bf16), 2).astype(f32)
    terms = [own[0]]
    for far in range(PANELS // 4 - 1, 0, -1):
        terms.append(swap(own[far].astype(bf16), 4 * far))
    return terms


def slot_places(routes, expert):
    tokens = routes.shape[1]
    matches = routes == expert
    hit = jnp.max(jnp.where(matches, 1.0, 0.0), axis=0, keepdims=True)
    earlier = lax.broadcasted_iota(jnp.int32, (tokens, tokens), 0) < lax.broadcasted_iota(
        jnp.int32, (tokens, tokens), 1
    )
    hits = jnp.broadcast_to(hit, (PAIR, tokens)).astype(bf16)
    order = jnp.dot(hits, jnp.where(earlier, 1.0, 0.0).astype(bf16), preferred_element_type=f32)
    slot = lax.broadcasted_iota(jnp.int32, (PAIR, tokens), 0) % CAP
    place = jnp.where((hit > 0.5) & (order.astype(jnp.int32) == slot), 1.0, 0.0)
    return matches, place


def slot_probs(matches, place, probs):
    route_prob = jnp.sum(jnp.where(matches, probs, 0.0), axis=0, keepdims=True)
    return jnp.sum(place * route_prob, axis=1, keepdims=True)


def pick_kernel(experts, routes_ref, probs_ref, tokens_ref, grads_ref, send_ref, place_ref, weight_ref):
    @pl.when(pl.program_id(0) == 0)
    def _():
        for e in range(experts):
            matches, place = slot_places(routes_ref[...], e)
            place_ref[e] = place.astype(bf16)
            weight_ref[e] = slot_probs(matches, place, probs_ref[...])

    for e in range(experts):
        place = place_ref[e]
        picked = jnp.dot(place, tokens_ref[...], preferred_element_type=f32)
        grads = jnp.dot(place, grads_ref[...], preferred_element_type=f32)
        is_token = lax.broadcasted_iota(jnp.int32, picked.shape, 0) < CAP
        send_ref[e] = jnp.where(is_token, picked, weight_ref[e] * grads).astype(bf16)


def pick(routes, probs, tokens, grads, experts):
    count, width = tokens.shape
    chunk = chunk_of(width, 1792)
    topk = routes.shape[0]
    whole = lambda i: (0, 0)
    return pl.pallas_call(
        functools.partial(pick_kernel, experts),
        grid=(width // chunk,),
        in_specs=[
            pl.BlockSpec((topk, count), whole),
            pl.BlockSpec((topk, count), whole),
            pl.BlockSpec((count, chunk), lambda i: (0, i)),
            pl.BlockSpec((count, chunk), lambda i: (0, i)),
        ],
        out_specs=pl.BlockSpec((experts, PAIR, chunk), lambda i: (0, 0, i)),
        out_shape=jax.ShapeDtypeStruct((experts, PAIR, width), bf16),
        scratch_shapes=[pltpu.VMEM((experts, PAIR, count), bf16), pltpu.VMEM((experts, PAIR, 1), f32)],
        compiler_params=pltpu.CompilerParams(vmem_limit_bytes=16 * MIB),
        cost_estimate=pl.CostEstimate(
            flops=4 * experts * PAIR * count * width, bytes_accessed=4 * count * width, transcendentals=0
        ),
        name="pick_rows",
    )(routes, probs, tokens, grads)


def expert_kernel(chunk, even_ref, odd_ref, gate_ref, up_ref, down_ref, even_out, odd_out):
    half, width = even_ref.shape
    count = 2 * half
    units = down_ref.shape[0]
    gate_pre = jnp.zeros((count, units), f32)
    up_pre = jnp.zeros((count, units), f32)
    hidden_grad = jnp.zeros((count, units), f32)
    for start in range(0, width, chunk):
        cols = slice(start, start + chunk)
        rows = jnp.concatenate([even_ref[:, cols], odd_ref[:, cols]], axis=0)
        gate_pre += jnp.dot(rows, gate_ref[cols, :], preferred_element_type=f32)
        up_pre += jnp.dot(rows, up_ref[cols, :], preferred_element_type=f32)
        hidden_grad += lax.dot_general(rows, down_ref[:, cols], NT, preferred_element_type=f32)
    is_token = lax.broadcasted_iota(jnp.int32, (count, units), 0) % PAIR < CAP
    hidden_grad = pltpu.roll(hidden_grad, count - CAP, 0)
    sigmoid_gate = jax.nn.sigmoid(gate_pre)
    silu_gate = gate_pre * sigmoid_gate
    hidden = silu_gate * up_pre
    silu_slope = sigmoid_gate * (1.0 + gate_pre * (1.0 - sigmoid_gate))
    gate_grad = pltpu.roll(hidden_grad * up_pre * silu_slope, CAP, 0)
    up_grad = pltpu.roll(hidden_grad * silu_gate, CAP, 0)
    hidden = jnp.where(is_token, hidden, 0.0).astype(bf16)
    gate_grad = jnp.where(is_token, 0.0, gate_grad).astype(bf16)
    up_grad = jnp.where(is_token, 0.0, up_grad).astype(bf16)
    for start in range(0, width, chunk):
        cols = slice(start, start + chunk)
        part = jnp.dot(hidden, down_ref[:, cols], preferred_element_type=f32)
        part += lax.dot_general(gate_grad, gate_ref[cols, :], NT, preferred_element_type=f32)
        part += lax.dot_general(up_grad, up_ref[cols, :], NT, preferred_element_type=f32)
        part = part.astype(bf16)
        even_out[:, cols] = part[:half]
        odd_out[:, cols] = part[half:]


def expert_rows(even, odd, w_gate, w_up, w_down):
    half, width = even.shape
    units = w_down.shape[0]
    vmem = pl.BlockSpec(memory_space=pltpu.VMEM)
    return pl.pallas_call(
        functools.partial(expert_kernel, chunk_of(width, 1024)),
        in_specs=[vmem] * 5,
        out_specs=[vmem] * 2,
        out_shape=[jax.ShapeDtypeStruct((half, width), bf16)] * 2,
        compiler_params=pltpu.CompilerParams(vmem_limit_bytes=40 * MIB),
        cost_estimate=pl.CostEstimate(
            flops=24 * half * width * units,
            bytes_accessed=6 * width * units + 8 * half * width,
            transcendentals=2 * half * units,
        ),
        name="expert_rows",
    )(even, odd, w_gate, w_up, w_down)


def thirds(x):
    high = x.astype(bf16)
    rest = x - high.astype(f32)
    middle = rest.astype(bf16)
    return high, middle, (rest - middle.astype(f32)).astype(bf16)


def finish_kernel(
    experts, n_terms, routes_ref, probs_ref, tokens_ref, grads_ref, *refs
):
    term_refs = refs[:n_terms]
    layer_ref, input_ref, prob_grad_ref, place_ref, weight_ref, dot_ref = refs[n_terms:]
    count = tokens_ref.shape[0]
    step = pl.program_id(0)

    @pl.when(step == 0)
    def _():
        for e in range(experts):
            matches, place = slot_places(routes_ref[...], e)
            place_ref[e] = place
            weight_ref[e] = slot_probs(matches, place, probs_ref[...])
            dot_ref[e] = jnp.zeros((PAIR, 1), f32)

    tokens = tokens_ref[...].astype(f32)
    grads = grads_ref[...].astype(f32)
    for e in range(experts):
        place = place_ref[e]
        total = term_refs[0][e].astype(f32)
        for ref in term_refs[1:]:
            total += ref[e].astype(f32)
        is_token = lax.broadcasted_iota(jnp.int32, total.shape, 0) < CAP
        mixed = jnp.where(is_token, weight_ref[e] * total, total)
        high, middle, low = thirds(mixed)
        values = jnp.concatenate([high.astype(f32), middle.astype(f32), low.astype(f32)], axis=0).astype(bf16)
        token_row = lax.broadcasted_iota(jnp.int32, place.shape, 0) < CAP
        to_layer = jnp.where(token_row, place, 0.0)
        to_input = jnp.where(token_row, 0.0, place)
        adder = jnp.concatenate([to_layer, to_input], axis=1)
        adder = jnp.concatenate([adder, adder, adder], axis=0).astype(bf16)
        added = lax.dot_general(adder, values, TN, preferred_element_type=f32)
        tokens += added[:count]
        grads += added[count:]
        grad_rows = jnp.dot(place.astype(bf16), grads_ref[...], preferred_element_type=f32)
        dot_ref[e] += jnp.sum(grad_rows * total, axis=1, keepdims=True)
    layer_ref[...] = tokens.astype(bf16)
    input_ref[...] = grads.astype(bf16)

    @pl.when(step == pl.num_programs(0) - 1)
    def _():
        result = jnp.zeros(routes_ref.shape, f32)
        for e in range(experts):
            token_row = lax.broadcasted_iota(jnp.int32, (PAIR, count), 0) < CAP
            token_dot = jnp.sum(jnp.where(token_row, place_ref[e] * dot_ref[e], 0.0), axis=0, keepdims=True)
            result += jnp.where(routes_ref[...] == e, token_dot, 0.0)
        prob_grad_ref[...] = result


def finish(routes, probs, tokens, grads, terms, experts):
    count, width = tokens.shape
    chunk = chunk_of(width, 1792)
    topk = routes.shape[0]
    whole = lambda i: (0, 0)
    across = pl.BlockSpec((count, chunk), lambda i: (0, i))
    return pl.pallas_call(
        functools.partial(finish_kernel, experts, len(terms)),
        grid=(width // chunk,),
        in_specs=[pl.BlockSpec((topk, count), whole), pl.BlockSpec((topk, count), whole), across, across]
        + [pl.BlockSpec((experts, PAIR, chunk), lambda i: (0, 0, i))] * len(terms),
        out_specs=[across, across, pl.BlockSpec((topk, count), whole)],
        out_shape=[
            jax.ShapeDtypeStruct((count, width), bf16),
            jax.ShapeDtypeStruct((count, width), bf16),
            jax.ShapeDtypeStruct((topk, count), f32),
        ],
        scratch_shapes=[
            pltpu.VMEM((experts, PAIR, count), f32),
            pltpu.VMEM((experts, PAIR, 1), f32),
            pltpu.VMEM((experts, PAIR, 1), f32),
        ],
        compiler_params=pltpu.CompilerParams(vmem_limit_bytes=32 * MIB),
        cost_estimate=pl.CostEstimate(
            flops=16 * experts * PAIR * count * width, bytes_accessed=8 * count * width, transcendentals=0
        ),
        name="finish",
    )(routes, probs, tokens, grads, *terms)


def local(tokens, out_grad, routes, gate_probs, w_gate, w_up, w_down):
    experts = lax.axis_size(AXIS) // PANELS
    width = tokens.shape[1]
    rows = PAIR * experts
    peers = [[e * PANELS + r for e in range(experts)] for r in range(PANELS)]
    send = pick(routes.T, gate_probs.T, tokens, out_grad, experts)
    if experts > 1:
        send = lax.all_to_all(send, AXIS, 0, 0, axis_index_groups=peers, tiled=True)
    even, odd = gather_rows(send.reshape(rows, width))
    even, odd = expert_rows(even, odd, w_gate, w_up, w_down)
    terms = scatter_sum(even, odd)
    if experts > 1:
        terms = [functools.reduce(jnp.add, [t.astype(f32) for t in terms])]
    terms = [t.reshape(experts, PAIR, width) for t in terms]
    if experts > 1:
        terms = [lax.all_to_all(terms[0], AXIS, 0, 0, axis_index_groups=peers, tiled=True)]
    layer_out, input_grad, prob_grad = finish(routes.T, gate_probs.T, tokens, out_grad, terms, experts)
    return layer_out, input_grad, prob_grad.T


def solution(mesh):
    rows = P(("groups", AXIS), None)
    return jax.shard_map(
        local,
        mesh=mesh,
        in_specs=(rows, rows, rows, rows, P(None, AXIS), P(None, AXIS), P(AXIS, None)),
        out_specs=(rows, rows, rows),
        check_vma=False,
    )
```

```python
import functools

import jax
import jax.numpy as jnp
from jax import lax
from jax.experimental import pallas as pl
from jax.experimental.pallas import tpu as pltpu
from jax.sharding import PartitionSpec as P

HID = 2048
PANEL = 128
CAP = 4
PANELS = HID // PANEL
PAIR = 2 * CAP
AXIS = "expert"
MIB = 1 << 20

f32 = jnp.float32
bf16 = jnp.bfloat16
NT = (((1,), (1,)), ((), ()))
TN = (((0,), (0,)), ((), ()))


def chunk_of(width, most):
    return max(c for c in range(128, most + 1, 128) if width % c == 0)


def swap(x, offset):
    devices = lax.axis_size(AXIS)
    return lax.ppermute(x, AXIS, [(i, i ^ offset) for i in range(devices)])


def gather_rows(x):
    blocks = {0: x}
    for far in range(PANELS // 4 - 1, 0, -1):
        blocks[4 * far] = swap(x, 4 * far)
    for far in range(PANELS // 4):
        blocks[4 * far + 2] = swap(blocks[4 * far], 2)
    even = jnp.concatenate([blocks[k] for k in range(0, PANELS, 2)], axis=0)
    return even, swap(even, 1)


def scatter_sum(even, odd):
    rows = even.shape[0] // (PANELS // 2)
    fars = range(PANELS // 4 - 1, -1, -1)
    part = (even.astype(f32) + swap(odd, 1).astype(f32)).reshape(PANELS // 2, rows, -1)
    kept = lax.optimization_barrier([part[2 * far] for far in fars])
    sent = lax.optimization_barrier([part[2 * far + 1].astype(bf16) for far in fars])
    terms = []
    for far, mine, other in zip(fars, kept, sent):
        own = mine + swap(other, 2).astype(f32)
        terms.append(swap(own.astype(bf16), 4 * far) if far else own)
    return terms[::-1]


def slot_places(routes, expert):
    tokens = routes.shape[1]
    matches = routes == expert
    hit = jnp.max(jnp.where(matches, 1.0, 0.0), axis=0, keepdims=True)
    earlier = lax.broadcasted_iota(jnp.int32, (tokens, tokens), 0) < lax.broadcasted_iota(
        jnp.int32, (tokens, tokens), 1
    )
    hits = jnp.broadcast_to(hit, (PAIR, tokens)).astype(bf16)
    order = jnp.dot(hits, jnp.where(earlier, 1.0, 0.0).astype(bf16), preferred_element_type=f32)
    slot = lax.broadcasted_iota(jnp.int32, (PAIR, tokens), 0) % CAP
    place = jnp.where((hit > 0.5) & (order.astype(jnp.int32) == slot), 1.0, 0.0)
    return matches, place


def slot_probs(matches, place, probs):
    route_prob = jnp.sum(jnp.where(matches, probs, 0.0), axis=0, keepdims=True)
    return jnp.sum(place * route_prob, axis=1, keepdims=True)


def pick_kernel(experts, chunk, routes_hbm, probs_hbm, tokens_hbm, grads_hbm, send_ref, *scratch):
    routes_ref, probs_ref, tokens_ref, grads_ref, small_sems, token_sems, grad_sems = scratch
    width = tokens_ref.shape[1]
    starts = range(0, width, chunk)
    small = [
        pltpu.make_async_copy(routes_hbm, routes_ref, small_sems.at[0]),
        pltpu.make_async_copy(probs_hbm, probs_ref, small_sems.at[1]),
    ]
    for copy in small:
        copy.start()
    large = []
    for i, start in enumerate(starts):
        cols = pl.ds(start, chunk)
        large.append(
            (
                pltpu.make_async_copy(tokens_hbm.at[:, cols], tokens_ref.at[:, cols], token_sems.at[i]),
                pltpu.make_async_copy(grads_hbm.at[:, cols], grads_ref.at[:, cols], grad_sems.at[i]),
            )
        )
        for copy in large[-1]:
            copy.start()
    for copy in small:
        copy.wait()
    places, weights = [], []
    for e in range(experts):
        matches, place = slot_places(routes_ref[...], e)
        places.append(place.astype(bf16))
        weights.append(slot_probs(matches, place, probs_ref[...]))
    for i, start in enumerate(starts):
        cols = slice(start, start + chunk)
        for copy in large[i]:
            copy.wait()
        for e in range(experts):
            picked = jnp.dot(places[e], tokens_ref[:, cols], preferred_element_type=f32)
            grads = jnp.dot(places[e], grads_ref[:, cols], preferred_element_type=f32)
            is_token = lax.broadcasted_iota(jnp.int32, picked.shape, 0) < CAP
            send_ref[e, :, cols] = jnp.where(is_token, picked, weights[e] * grads).astype(bf16)


def pick(routes, probs, tokens, grads, experts):
    count, width = tokens.shape
    chunk = chunk_of(width, 1792)
    topk = routes.shape[0]
    hbm = pl.BlockSpec(memory_space=pltpu.HBM)
    return pl.pallas_call(
        functools.partial(pick_kernel, experts, chunk),
        in_specs=[hbm] * 4,
        out_specs=pl.BlockSpec(memory_space=pltpu.VMEM),
        out_shape=jax.ShapeDtypeStruct((experts, PAIR, width), bf16),
        scratch_shapes=[
            pltpu.VMEM((topk, count), routes.dtype),
            pltpu.VMEM((topk, count), probs.dtype),
            pltpu.VMEM((count, width), bf16),
            pltpu.VMEM((count, width), bf16),
            pltpu.SemaphoreType.DMA((2,)),
            pltpu.SemaphoreType.DMA((width // chunk,)),
            pltpu.SemaphoreType.DMA((width // chunk,)),
        ],
        compiler_params=pltpu.CompilerParams(vmem_limit_bytes=16 * MIB),
        cost_estimate=pl.CostEstimate(
            flops=4 * experts * PAIR * count * width, bytes_accessed=4 * count * width, transcendentals=0
        ),
        name="pick_rows",
    )(*[pltpu.with_memory_space_constraint(x, pltpu.HBM) for x in (routes, probs, tokens, grads)])


def expert_kernel(chunk, even_ref, odd_ref, gate_ref, up_ref, down_ref, even_out, odd_out):
    half, width = even_ref.shape
    count = 2 * half
    units = down_ref.shape[0]
    both_pre = jnp.zeros((count, 2 * units), f32)
    hidden_grad = jnp.zeros((count, units), f32)
    for start in range(0, width, chunk):
        cols = slice(start, start + chunk)
        rows = jnp.concatenate([even_ref[:, cols], odd_ref[:, cols]], axis=0)
        both = jnp.concatenate([gate_ref[cols, :], up_ref[cols, :]], axis=1)
        both_pre += jnp.dot(rows, both, preferred_element_type=f32)
        hidden_grad += lax.dot_general(rows, down_ref[:, cols], NT, preferred_element_type=f32)
    is_token = lax.broadcasted_iota(jnp.int32, (count, units), 0) % PAIR < CAP
    gate_pre, up_pre = both_pre[:, :units], both_pre[:, units:]
    hidden_grad = pltpu.roll(hidden_grad, count - CAP, 0)
    sigmoid_gate = jax.nn.sigmoid(gate_pre)
    silu_gate = gate_pre * sigmoid_gate
    hidden = silu_gate * up_pre
    silu_slope = sigmoid_gate * (1.0 + gate_pre * (1.0 - sigmoid_gate))
    gate_grad = pltpu.roll(hidden_grad * up_pre * silu_slope, CAP, 0)
    up_grad = pltpu.roll(hidden_grad * silu_gate, CAP, 0)
    hidden = jnp.where(is_token, hidden, 0.0).astype(bf16)
    gate_grad = jnp.where(is_token, 0.0, gate_grad).astype(bf16)
    up_grad = jnp.where(is_token, 0.0, up_grad).astype(bf16)
    both_grad = jnp.concatenate([gate_grad, up_grad], axis=1)
    for start in range(0, width, chunk):
        cols = slice(start, start + chunk)
        part = jnp.dot(hidden, down_ref[:, cols], preferred_element_type=f32)
        both = jnp.concatenate([gate_ref[cols, :], up_ref[cols, :]], axis=1)
        part += lax.dot_general(both_grad, both, NT, preferred_element_type=f32)
        part = part.astype(bf16)
        even_out[:, cols] = part[:half]
        odd_out[:, cols] = part[half:]


def expert_rows(even, odd, w_gate, w_up, w_down):
    half, width = even.shape
    units = w_down.shape[0]
    vmem = pl.BlockSpec(memory_space=pltpu.VMEM)
    return pl.pallas_call(
        functools.partial(expert_kernel, chunk_of(width, 1024)),
        in_specs=[vmem] * 5,
        out_specs=[vmem] * 2,
        out_shape=[jax.ShapeDtypeStruct((half, width), bf16)] * 2,
        compiler_params=pltpu.CompilerParams(vmem_limit_bytes=40 * MIB),
        cost_estimate=pl.CostEstimate(
            flops=24 * half * width * units,
            bytes_accessed=6 * width * units + 8 * half * width,
            transcendentals=2 * half * units,
        ),
        name="expert_rows",
    )(even, odd, w_gate, w_up, w_down)


def thirds(x):
    high = x.astype(bf16)
    rest = x - high.astype(f32)
    middle = rest.astype(bf16)
    return high, middle, (rest - middle.astype(f32)).astype(bf16)


def finish_kernel(
    experts, n_terms, routes_ref, probs_ref, tokens_ref, grads_ref, *refs
):
    term_refs = refs[:n_terms]
    layer_ref, input_ref, prob_grad_ref, place_ref, weight_ref, dot_ref = refs[n_terms:]
    count = tokens_ref.shape[0]
    step = pl.program_id(0)

    @pl.when(step == 0)
    def _():
        for e in range(experts):
            matches, place = slot_places(routes_ref[...], e)
            place_ref[e] = place
            weight_ref[e] = slot_probs(matches, place, probs_ref[...])
            dot_ref[e] = jnp.zeros((PAIR, 1), f32)

    tokens = tokens_ref[...].astype(f32)
    grads = grads_ref[...].astype(f32)
    for e in range(experts):
        place = place_ref[e]
        total = term_refs[0][e].astype(f32)
        for ref in term_refs[1:]:
            total += ref[e].astype(f32)
        is_token = lax.broadcasted_iota(jnp.int32, total.shape, 0) < CAP
        mixed = jnp.where(is_token, weight_ref[e] * total, total)
        high, middle, low = thirds(mixed)
        values = jnp.concatenate([high.astype(f32), middle.astype(f32), low.astype(f32)], axis=0).astype(bf16)
        token_row = lax.broadcasted_iota(jnp.int32, place.shape, 0) < CAP
        to_layer = jnp.where(token_row, place, 0.0)
        to_input = jnp.where(token_row, 0.0, place)
        adder = jnp.concatenate([to_layer, to_input], axis=1)
        adder = jnp.concatenate([adder, adder, adder], axis=0).astype(bf16)
        added = lax.dot_general(adder, values, TN, preferred_element_type=f32)
        tokens += added[:count]
        grads += added[count:]
        grad_rows = jnp.dot(place.astype(bf16), grads_ref[...], preferred_element_type=f32)
        dot_ref[e] += jnp.sum(grad_rows * total, axis=1, keepdims=True)
    layer_ref[...] = tokens.astype(bf16)
    input_ref[...] = grads.astype(bf16)

    @pl.when(step == pl.num_programs(0) - 1)
    def _():
        result = jnp.zeros(routes_ref.shape, f32)
        for e in range(experts):
            token_row = lax.broadcasted_iota(jnp.int32, (PAIR, count), 0) < CAP
            token_dot = jnp.sum(jnp.where(token_row, place_ref[e] * dot_ref[e], 0.0), axis=0, keepdims=True)
            result += jnp.where(routes_ref[...] == e, token_dot, 0.0)
        prob_grad_ref[...] = result


def finish(routes, probs, tokens, grads, terms, experts):
    count, width = tokens.shape
    chunk = chunk_of(width, 1792)
    topk = routes.shape[0]
    whole = lambda i: (0, 0)
    across = pl.BlockSpec((count, chunk), lambda i: (0, i))
    return pl.pallas_call(
        functools.partial(finish_kernel, experts, len(terms)),
        grid=(width // chunk,),
        in_specs=[pl.BlockSpec((topk, count), whole), pl.BlockSpec((topk, count), whole), across, across]
        + [pl.BlockSpec((experts, PAIR, chunk), lambda i: (0, 0, i))] * len(terms),
        out_specs=[across, across, pl.BlockSpec((topk, count), whole)],
        out_shape=[
            jax.ShapeDtypeStruct((count, width), bf16),
            jax.ShapeDtypeStruct((count, width), bf16),
            jax.ShapeDtypeStruct((topk, count), f32),
        ],
        scratch_shapes=[
            pltpu.VMEM((experts, PAIR, count), f32),
            pltpu.VMEM((experts, PAIR, 1), f32),
            pltpu.VMEM((experts, PAIR, 1), f32),
        ],
        compiler_params=pltpu.CompilerParams(vmem_limit_bytes=32 * MIB),
        cost_estimate=pl.CostEstimate(
            flops=16 * experts * PAIR * count * width, bytes_accessed=8 * count * width, transcendentals=0
        ),
        name="finish",
    )(routes, probs, tokens, grads, *terms)


def local(tokens, out_grad, routes, gate_probs, w_gate, w_up, w_down):
    experts = lax.axis_size(AXIS) // PANELS
    width = tokens.shape[1]
    rows = PAIR * experts
    peers = [[e * PANELS + r for e in range(experts)] for r in range(PANELS)]
    send = pick(routes.T, gate_probs.T, tokens, out_grad, experts)
    if experts > 1:
        send = lax.all_to_all(send, AXIS, 0, 0, axis_index_groups=peers, tiled=True)
    even, odd = gather_rows(send.reshape(rows, width))
    even, odd = expert_rows(even, odd, w_gate, w_up, w_down)
    terms = scatter_sum(even, odd)
    if experts > 1:
        terms = [functools.reduce(jnp.add, [t.astype(f32) for t in terms])]
    terms = [t.reshape(experts, PAIR, width) for t in terms]
    if experts > 1:
        terms = [lax.all_to_all(terms[0], AXIS, 0, 0, axis_index_groups=peers, tiled=True)]
    layer_out, input_grad, prob_grad = finish(routes.T, gate_probs.T, tokens, out_grad, terms, experts)
    return layer_out, input_grad, prob_grad.T


def solution(mesh):
    rows = P(("groups", AXIS), None)
    return jax.shard_map(
        local,
        mesh=mesh,
        in_specs=(rows, rows, rows, rows, P(None, AXIS), P(None, AXIS), P(AXIS, None)),
        out_specs=(rows, rows, rows),
        check_vma=False,
    )
```

```python
import functools

import jax
import jax.numpy as jnp
from jax import lax
from jax.experimental import pallas as pl
from jax.experimental.pallas import tpu as pltpu
from jax.sharding import PartitionSpec as P

HID = 2048
PANEL = 128
CAP = 4
PANELS = HID // PANEL
PAIR = 2 * CAP
AXIS = "expert"
MIB = 1 << 20
VMEM = pl.BlockSpec(memory_space=pltpu.VMEM)
ANY = pl.BlockSpec(memory_space=pl.ANY)

f32 = jnp.float32
bf16 = jnp.bfloat16
NT = (((1,), (1,)), ((), ()))
TN = (((0,), (0,)), ((), ()))


def chunk_of(width, most):
    return max(c for c in range(128, most + 1, 128) if width % c == 0)


def swap(x, offset):
    devices = lax.axis_size(AXIS)
    return lax.ppermute(x, AXIS, [(i, i ^ offset) for i in range(devices)])


NEAR = (0, 2, 4, 6)
FAR = 8


def stack_kernel(chunk, count, *refs):
    block_refs, out_ref = refs[:count], refs[-1]
    for start in range(0, out_ref.shape[1], chunk):
        cols = slice(start, start + chunk)
        blocks = [ref[:, cols].astype(f32) for ref in block_refs]
        out_ref[:, cols] = jnp.concatenate(blocks, axis=0).astype(bf16)


def stack_rows(blocks, *after):
    rows, width = blocks[0].shape
    return pl.pallas_call(
        functools.partial(stack_kernel, chunk_of(width, 1024), len(blocks)),
        in_specs=[VMEM] * len(blocks) + [ANY] * len(after),
        out_specs=VMEM,
        out_shape=jax.ShapeDtypeStruct((len(blocks) * rows, width), bf16),
        compiler_params=pltpu.CompilerParams(vmem_limit_bytes=16 * MIB),
        cost_estimate=pl.CostEstimate(
            flops=0, bytes_accessed=4 * len(blocks) * rows * width, transcendentals=0
        ),
        name="stack_rows",
    )(*blocks, *after)


def slot_places(routes, expert):
    tokens = routes.shape[1]
    matches = routes == expert
    hit = jnp.max(jnp.where(matches, 1.0, 0.0), axis=0, keepdims=True)
    earlier = lax.broadcasted_iota(jnp.int32, (tokens, tokens), 0) < lax.broadcasted_iota(
        jnp.int32, (tokens, tokens), 1
    )
    hits = jnp.broadcast_to(hit, (PAIR, tokens)).astype(bf16)
    order = jnp.dot(hits, jnp.where(earlier, 1.0, 0.0).astype(bf16), preferred_element_type=f32)
    slot = lax.broadcasted_iota(jnp.int32, (PAIR, tokens), 0) % CAP
    place = jnp.where((hit > 0.5) & (order.astype(jnp.int32) == slot), 1.0, 0.0)
    return matches, place


def slot_probs(matches, place, probs):
    route_prob = jnp.sum(jnp.where(matches, probs, 0.0), axis=0, keepdims=True)
    return jnp.sum(place * route_prob, axis=1, keepdims=True)


def pick_kernel(experts, chunk, routes_hbm, probs_hbm, tokens_hbm, grads_hbm, send_ref, *scratch):
    routes_ref, probs_ref, tokens_ref, grads_ref, small_sems, token_sems, grad_sems = scratch
    width = tokens_ref.shape[1]
    starts = range(0, width, chunk)
    small = [
        pltpu.make_async_copy(routes_hbm, routes_ref, small_sems.at[0]),
        pltpu.make_async_copy(probs_hbm, probs_ref, small_sems.at[1]),
    ]
    for copy in small:
        copy.start()
    large = []
    for i, start in enumerate(starts):
        cols = pl.ds(start, chunk)
        large.append(
            (
                pltpu.make_async_copy(tokens_hbm.at[:, cols], tokens_ref.at[:, cols], token_sems.at[i]),
                pltpu.make_async_copy(grads_hbm.at[:, cols], grads_ref.at[:, cols], grad_sems.at[i]),
            )
        )
        for copy in large[-1]:
            copy.start()
    for copy in small:
        copy.wait()
    places, weights = [], []
    for e in range(experts):
        matches, place = slot_places(routes_ref[...], e)
        places.append(place.astype(bf16))
        weights.append(slot_probs(matches, place, probs_ref[...]))
    for i, start in enumerate(starts):
        cols = slice(start, start + chunk)
        for copy in large[i]:
            copy.wait()
        for e in range(experts):
            picked = jnp.dot(places[e], tokens_ref[:, cols], preferred_element_type=f32)
            grads = jnp.dot(places[e], grads_ref[:, cols], preferred_element_type=f32)
            is_token = lax.broadcasted_iota(jnp.int32, picked.shape, 0) < CAP
            send_ref[e, :, cols] = jnp.where(is_token, picked, weights[e] * grads).astype(bf16)


def pick(routes, probs, tokens, grads, experts):
    count, width = tokens.shape
    chunk = chunk_of(width, 1792)
    topk = routes.shape[0]
    hbm = pl.BlockSpec(memory_space=pltpu.HBM)
    return pl.pallas_call(
        functools.partial(pick_kernel, experts, chunk),
        in_specs=[hbm] * 4,
        out_specs=pl.BlockSpec(memory_space=pltpu.VMEM),
        out_shape=jax.ShapeDtypeStruct((experts, PAIR, width), bf16),
        scratch_shapes=[
            pltpu.VMEM((topk, count), routes.dtype),
            pltpu.VMEM((topk, count), probs.dtype),
            pltpu.VMEM((count, width), bf16),
            pltpu.VMEM((count, width), bf16),
            pltpu.SemaphoreType.DMA((2,)),
            pltpu.SemaphoreType.DMA((width // chunk,)),
            pltpu.SemaphoreType.DMA((width // chunk,)),
        ],
        compiler_params=pltpu.CompilerParams(vmem_limit_bytes=16 * MIB),
        cost_estimate=pl.CostEstimate(
            flops=4 * experts * PAIR * count * width, bytes_accessed=4 * count * width, transcendentals=0
        ),
        name="pick_rows",
    )(*[pltpu.with_memory_space_constraint(x, pltpu.HBM) for x in (routes, probs, tokens, grads)])


def hidden_rows(chunk, row_refs, gate_ref, up_ref, down_ref):
    half, width = row_refs[0].shape
    parts = slice(0, half // 2), slice(half // 2, half)
    count = 2 * half
    units = down_ref.shape[0]
    both_pre = jnp.zeros((count, 2 * units), f32)
    hidden_grad = jnp.zeros((count, units), f32)
    for start in range(0, width, chunk):
        cols = slice(start, start + chunk)
        rows = jnp.concatenate([ref[part, cols] for part in parts for ref in row_refs], axis=0)
        both = jnp.concatenate([gate_ref[cols, :], up_ref[cols, :]], axis=1)
        both_pre += jnp.dot(rows, both, preferred_element_type=f32)
        hidden_grad += lax.dot_general(rows, down_ref[:, cols], NT, preferred_element_type=f32)
    is_token = lax.broadcasted_iota(jnp.int32, (count, units), 0) % PAIR < CAP
    gate_pre, up_pre = both_pre[:, :units], both_pre[:, units:]
    hidden_grad = pltpu.roll(hidden_grad, count - CAP, 0)
    sigmoid_gate = jax.nn.sigmoid(gate_pre)
    silu_gate = gate_pre * sigmoid_gate
    hidden = silu_gate * up_pre
    silu_slope = sigmoid_gate * (1.0 + gate_pre * (1.0 - sigmoid_gate))
    gate_grad = pltpu.roll(hidden_grad * up_pre * silu_slope, CAP, 0)
    up_grad = pltpu.roll(hidden_grad * silu_gate, CAP, 0)
    hidden = jnp.where(is_token, hidden, 0.0).astype(bf16)
    gate_grad = jnp.where(is_token, 0.0, gate_grad).astype(bf16)
    up_grad = jnp.where(is_token, 0.0, up_grad).astype(bf16)
    return hidden, jnp.concatenate([gate_grad, up_grad], axis=1)


def panel_rows(chunk, hidden, both_grad, gate_ref, up_ref, down_ref, even_out, odd_out):
    half, width = even_out.shape
    for start in range(0, width, chunk):
        cols = slice(start, start + chunk)
        part = jnp.dot(hidden, down_ref[:, cols], preferred_element_type=f32)
        both = jnp.concatenate([gate_ref[cols, :], up_ref[cols, :]], axis=1)
        part += lax.dot_general(both_grad, both, NT, preferred_element_type=f32)
        odd_out[:, cols] = part[half:].astype(bf16)
        even_out[:, cols] = part[:half]


def first_kernel(chunk, *refs):
    even_ref, odd_ref, gate_ref, up_ref, down_ref, even_out, odd_out, hidden_out, both_out = refs
    hidden, both_grad = hidden_rows(chunk, (even_ref, odd_ref), gate_ref, up_ref, down_ref)
    far = hidden.shape[0] // 2
    hidden_out[...], both_out[...] = hidden[far:], both_grad[far:]
    panel_rows(chunk, hidden[:far], both_grad[:far], gate_ref, up_ref, down_ref, even_out, odd_out)


def second_kernel(chunk, hidden_ref, both_ref, gate_ref, up_ref, down_ref, even_out, odd_out):
    panel_rows(chunk, hidden_ref[...], both_ref[...], gate_ref, up_ref, down_ref, even_out, odd_out)


def expert_call(kernel, name, operands, out_shape, flops):
    return pl.pallas_call(
        functools.partial(kernel, chunk_of(out_shape[0].shape[1], 1024)),
        in_specs=[VMEM] * len(operands),
        out_specs=[VMEM] * len(out_shape),
        out_shape=out_shape,
        compiler_params=pltpu.CompilerParams(vmem_limit_bytes=24 * MIB),
        cost_estimate=pl.CostEstimate(
            flops=flops, bytes_accessed=sum(2 * x.size for x in operands), transcendentals=0
        ),
        name=name,
    )(*operands)


def expert_far(even, odd, weights):
    count, width = even.shape
    units = weights[2].shape[0]
    out_shape = [
        jax.ShapeDtypeStruct((count // 2, width), f32),
        jax.ShapeDtypeStruct((count // 2, width), bf16),
        jax.ShapeDtypeStruct((count, units), bf16),
        jax.ShapeDtypeStruct((count, 2 * units), bf16),
    ]
    flops = 18 * count * width * units
    return expert_call(first_kernel, "expert_far", (even, odd, *weights), out_shape, flops)


def expert_near(hidden, both_grad, weights):
    count, units = hidden.shape
    width = weights[2].shape[1]
    out_shape = [
        jax.ShapeDtypeStruct((count // 2, width), f32),
        jax.ShapeDtypeStruct((count // 2, width), bf16),
    ]
    flops = 6 * count * width * units
    return expert_call(second_kernel, "expert_near", (hidden, both_grad, *weights), out_shape, flops)


def sum_kernel(chunk, even_ref, odd_ref, after_ref, kept_ref, *sent_refs):
    del after_ref
    rows, width = kept_ref.shape
    for start in range(0, width, chunk):
        cols = slice(start, start + chunk)
        total = even_ref[:, cols] + odd_ref[:, cols].astype(f32)
        kept_ref[:, cols] = total[:rows]
        for i, ref in enumerate(sent_refs):
            ref[:, cols] = total[(i + 1) * rows : (i + 2) * rows].astype(bf16)


def sum_blocks(even, odd, after):
    count, width = even.shape
    rows = count // len(NEAR)
    return pl.pallas_call(
        functools.partial(sum_kernel, chunk_of(width, 1024)),
        in_specs=[VMEM] * 2 + [ANY],
        out_specs=[VMEM] * len(NEAR),
        out_shape=[jax.ShapeDtypeStruct((rows, width), f32)]
        + [jax.ShapeDtypeStruct((rows, width), bf16)] * (len(NEAR) - 1),
        compiler_params=pltpu.CompilerParams(vmem_limit_bytes=16 * MIB),
        cost_estimate=pl.CostEstimate(flops=count * width, bytes_accessed=8 * count * width, transcendentals=0),
        name="sum_blocks",
    )(even, odd, after)


def exchange(send, weights):
    by_4 = stack_rows([swap(send, 4)], send)
    far = stack_rows([swap(send, FAR)], by_4)
    blocks = [far] + [swap(far, k) for k in NEAR[1:]] + [send, swap(send, 2), by_4, swap(by_4, 2)]
    even = stack_rows(blocks)
    far_even, far_odd, *near = expert_far(even, swap(even, 1), weights)
    near_even, near_odd = expert_near(*near, weights)

    kept_far, *sent_far = sum_blocks(far_even, swap(far_odd, 1), far_odd)
    total_far = kept_far
    for k in (6, 2, 4):
        total_far = total_far + swap(sent_far[NEAR.index(k) - 1], k).astype(f32)
    kept, for_2, for_4, for_6 = sum_blocks(near_even, swap(near_odd, 1), kept_far)
    for_4 = (for_4.astype(f32) + swap(for_6, 2).astype(f32)).astype(bf16)
    for_2 = stack_rows([for_2], for_4)
    return [kept, swap(for_2, 2), swap(for_4, 4), swap(total_far.astype(bf16), FAR)]


def thirds(x):
    high = x.astype(bf16)
    rest = x - high.astype(f32)
    middle = rest.astype(bf16)
    return high, middle, (rest - middle.astype(f32)).astype(bf16)


def finish_kernel(
    experts, n_terms, routes_ref, probs_ref, tokens_ref, grads_ref, *refs
):
    term_refs = refs[:n_terms]
    layer_ref, input_ref, prob_grad_ref, place_ref, weight_ref, dot_ref = refs[n_terms:]
    count = tokens_ref.shape[0]
    step = pl.program_id(0)

    @pl.when(step == 0)
    def _():
        for e in range(experts):
            matches, place = slot_places(routes_ref[...], e)
            place_ref[e] = place
            weight_ref[e] = slot_probs(matches, place, probs_ref[...])
            dot_ref[e] = jnp.zeros((PAIR, 1), f32)

    tokens = tokens_ref[...].astype(f32)
    grads = grads_ref[...].astype(f32)
    for e in range(experts):
        place = place_ref[e]
        total = term_refs[0][e].astype(f32)
        for ref in term_refs[1:]:
            total += ref[e].astype(f32)
        is_token = lax.broadcasted_iota(jnp.int32, total.shape, 0) < CAP
        mixed = jnp.where(is_token, weight_ref[e] * total, total)
        high, middle, low = thirds(mixed)
        values = jnp.concatenate([high.astype(f32), middle.astype(f32), low.astype(f32)], axis=0).astype(bf16)
        token_row = lax.broadcasted_iota(jnp.int32, place.shape, 0) < CAP
        to_layer = jnp.where(token_row, place, 0.0)
        to_input = jnp.where(token_row, 0.0, place)
        adder = jnp.concatenate([to_layer, to_input], axis=1)
        adder = jnp.concatenate([adder, adder, adder], axis=0).astype(bf16)
        added = lax.dot_general(adder, values, TN, preferred_element_type=f32)
        tokens += added[:count]
        grads += added[count:]
        grad_rows = jnp.dot(place.astype(bf16), grads_ref[...], preferred_element_type=f32)
        dot_ref[e] += jnp.sum(grad_rows * total, axis=1, keepdims=True)
    layer_ref[...] = tokens.astype(bf16)
    input_ref[...] = grads.astype(bf16)

    @pl.when(step == pl.num_programs(0) - 1)
    def _():
        result = jnp.zeros(routes_ref.shape, f32)
        for e in range(experts):
            token_row = lax.broadcasted_iota(jnp.int32, (PAIR, count), 0) < CAP
            token_dot = jnp.sum(jnp.where(token_row, place_ref[e] * dot_ref[e], 0.0), axis=0, keepdims=True)
            result += jnp.where(routes_ref[...] == e, token_dot, 0.0)
        prob_grad_ref[...] = result


def finish(routes, probs, tokens, grads, terms, experts):
    count, width = tokens.shape
    chunk = chunk_of(width, 1792)
    topk = routes.shape[0]
    whole = lambda i: (0, 0)
    across = pl.BlockSpec((count, chunk), lambda i: (0, i))
    return pl.pallas_call(
        functools.partial(finish_kernel, experts, len(terms)),
        grid=(width // chunk,),
        in_specs=[pl.BlockSpec((topk, count), whole), pl.BlockSpec((topk, count), whole), across, across]
        + [pl.BlockSpec((experts, PAIR, chunk), lambda i: (0, 0, i))] * len(terms),
        out_specs=[across, across, pl.BlockSpec((topk, count), whole)],
        out_shape=[
            jax.ShapeDtypeStruct((count, width), bf16),
            jax.ShapeDtypeStruct((count, width), bf16),
            jax.ShapeDtypeStruct((topk, count), f32),
        ],
        scratch_shapes=[
            pltpu.VMEM((experts, PAIR, count), f32),
            pltpu.VMEM((experts, PAIR, 1), f32),
            pltpu.VMEM((experts, PAIR, 1), f32),
        ],
        compiler_params=pltpu.CompilerParams(vmem_limit_bytes=32 * MIB),
        cost_estimate=pl.CostEstimate(
            flops=16 * experts * PAIR * count * width, bytes_accessed=8 * count * width, transcendentals=0
        ),
        name="finish",
    )(routes, probs, tokens, grads, *terms)


def local(tokens, out_grad, routes, gate_probs, w_gate, w_up, w_down):
    experts = lax.axis_size(AXIS) // PANELS
    width = tokens.shape[1]
    rows = PAIR * experts
    peers = [[e * PANELS + r for e in range(experts)] for r in range(PANELS)]
    send = pick(routes.T, gate_probs.T, tokens, out_grad, experts)
    if experts > 1:
        send = lax.all_to_all(send, AXIS, 0, 0, axis_index_groups=peers, tiled=True)
    terms = exchange(send.reshape(rows, width), (w_gate, w_up, w_down))
    if experts > 1:
        terms = [functools.reduce(jnp.add, [t.astype(f32) for t in terms])]
    terms = [t.reshape(experts, PAIR, width) for t in terms]
    if experts > 1:
        terms = [lax.all_to_all(terms[0], AXIS, 0, 0, axis_index_groups=peers, tiled=True)]
    layer_out, input_grad, prob_grad = finish(routes.T, gate_probs.T, tokens, out_grad, terms, experts)
    return layer_out, input_grad, prob_grad.T


def solution(mesh):
    rows = P(("groups", AXIS), None)
    return jax.shard_map(
        local,
        mesh=mesh,
        in_specs=(rows, rows, rows, rows, P(None, AXIS), P(None, AXIS), P(AXIS, None)),
        out_specs=(rows, rows, rows),
        check_vma=False,
    )
```
